256 devices in a mesh: ctx: 128 (over y_lo, x, z, core), head: 2 (over y_hi).
Axes of the slice: x: 4, y: 4 (y_hi: 2, y_lo: 2; y = y_hi * 2 + y_lo), z: 8, core: 2. Of those that a mesh axis runs over, the one named last changes fastest.
Arguments:
- queries: bfloat16 [32768, 4096], P(('ctx', 'head')), may hold values from -150 to 150
- keys: bfloat16 [32768, 1024], P(('ctx', 'head')), may hold values from -6 to 6
- values: bfloat16 [32768, 1024], P(('ctx', 'head')), may hold values from -6 to 6
- block_place: int32 [256], replicated, may hold values from 0 to 255, each once
Outputs:
- attention: bfloat16 [32768, 4096], P(('ctx', 'head'))
The draws below stay inside these ranges and needn't reach their ends.
Inputs may be any that keep to these rules, and one draw needn't show every extreme that they name: `block_place`: each of 0 to 255 appears once.
All inputs are finite; a program needn't handle non-finite values.
Results may differ from the reference program's by a relative error of at most 0.0037.
Values may be sent and summed in bfloat16 or wider, within the bound.
No kernel may reach another device: no remote copies, remote signals or barrier semaphores. Data moves between devices by JAX's collectives and lax.ppermute only.
A program may use at most 128 MiB of HBM per device.

```python
import jax
import jax.numpy as jnp
from jax import lax

HEADS = 32
KV_HEADS = 8
HEAD_DIM = 128
TOK_DEV = 256
WINDOW_STEPS = 3
SEQ = 32768
BLOCKS = 256
N_CTX = 128


def shared_keys(key):
    base = jax.random.normal(jax.random.fold_in(key, 101), (SEQ, KV_HEADS * HEAD_DIM), jnp.float32)
    return jnp.clip(base, -6.0, 6.0)


def draw_keys(key, part):
    base = shared_keys(key)
    return base.astype(jnp.bfloat16)


def draw_queries(key, part):
    key = jax.random.fold_in(key, 13)
    own = jnp.clip(jax.random.normal(key, (SEQ, HEADS * HEAD_DIM), jnp.float32), -6.0, 6.0)
    return own.astype(jnp.bfloat16)


def levels(key, shape, shards, least, largest):
    def one(position, blocks):
        steps = jax.random.uniform(jax.random.fold_in(jax.random.fold_in(key, 6), position), (blocks,), jnp.float32, least / len(shards), largest / len(shards))
        return jnp.repeat(jnp.exp(steps), shape[position] // blocks).reshape((-1,) + (1,) * (len(shape) - position - 1))

    level = one(*shards[0])
    for cut in shards[1:]:
        level = level * one(*cut)
    return level


def normal_values(rng, dims, spread, bound, split=(), kind=jnp.bfloat16):
    gain = levels(rng, dims, split, -0.22, 0.18) if split else 1.0
    drawn = jax.random.normal(rng, dims, jnp.float32) * spread * gain
    return jnp.minimum(jnp.maximum(drawn, -bound), bound).astype(kind)


def setup_inputs(seed: int = 0) -> dict:
    splits = jax.random.split(jax.random.key(seed), 5)
    queries = draw_queries(jax.random.fold_in(splits[4], 71), 0)
    keys = draw_keys(jax.random.fold_in(splits[4], 71), 0)
    values = normal_values(splits[2], (SEQ, KV_HEADS * HEAD_DIM), 1.0, 6.0, ((0, 256),))
    block_place = jax.random.permutation(splits[3], BLOCKS).astype(jnp.int32)
    return {"queries": queries, "keys": keys, "values": values, "block_place": block_place}


NEGATIVE = -1e30


def tile_part(q_half, k_half, v_half, q_place, k_place):
    rows = q_half.shape[0]
    groups = k_half.shape[1] // HEAD_DIM
    share = q_half.shape[1] // k_half.shape[1]
    q_four = q_half.astype(jnp.float32).reshape(rows, groups, share, HEAD_DIM)
    k_three = k_half.astype(jnp.float32).reshape(rows, groups, HEAD_DIM)
    v_three = v_half.astype(jnp.float32).reshape(rows, groups, HEAD_DIM)
    scores = jnp.einsum("agrd,bgd->grab", q_four, k_three, precision=lax.Precision.HIGHEST) * (HEAD_DIM ** -0.5)
    offsets = jnp.arange(rows, dtype=jnp.int32)
    visible = (k_place * rows + offsets)[None, :] <= (q_place * rows + offsets)[:, None]
    peak = jnp.max(jnp.where(visible, scores, NEGATIVE), axis=-1)
    weights = jnp.exp(jnp.where(visible, scores - peak[..., None], NEGATIVE))
    total = jnp.sum(weights, axis=-1)
    rounded = weights.astype(jnp.bfloat16).astype(jnp.float32)
    output = jnp.einsum("grab,bgd->agrd", rounded, v_three, precision=lax.Precision.HIGHEST)
    return output.reshape(rows, -1), peak.reshape(-1, rows), total.reshape(-1, rows)


def combine(first, second):
    out_a, peak_a, sum_a = first
    out_b, peak_b, sum_b = second
    peak = jnp.maximum(peak_a, peak_b)
    scale_a = jnp.exp(peak_a - peak)
    scale_b = jnp.exp(peak_b - peak)
    rows = out_a.shape[0]
    heads = peak.shape[0]
    mixed = out_a.reshape(rows, heads, -1) * scale_a.T[:, :, None] + out_b.reshape(rows, heads, -1) * scale_b.T[:, :, None]
    return mixed.reshape(rows, -1), peak, sum_a * scale_a + sum_b * scale_b


def block_part(q_block, q_pair, k_block, v_block, k_pair):
    half = q_block.shape[0] // 2
    results = []
    for first in range(2):
        merged = None
        for second in range(2):
            part = tile_part(q_block[first * half:(first + 1) * half], k_block[second * half:(second + 1) * half], v_block[second * half:(second + 1) * half], q_pair[first], k_pair[second])
            merged = part if merged is None else combine(merged, part)
        results.append(merged)
    return (jnp.concatenate([results[0][0], results[1][0]], axis=0), jnp.concatenate([results[0][1], results[1][1]], axis=1), jnp.concatenate([results[0][2], results[1][2]], axis=1))


def reference(queries, keys, values, block_place):
    q_blocks = queries.reshape(N_CTX, TOK_DEV, -1)
    k_blocks = keys.reshape(N_CTX, TOK_DEV, -1)
    v_blocks = values.reshape(N_CTX, TOK_DEV, -1)
    pairs = block_place.reshape(N_CTX, 2)

    def one_block(index):
        q_pair = pairs[index]
        merged = None
        for step in range(WINDOW_STEPS + 1):
            other = ((index + step) % N_CTX).astype(jnp.int32)
            part = block_part(q_blocks[index], q_pair, k_blocks[other], v_blocks[other], pairs[other])
            merged = part if merged is None else combine(merged, part)
        out_block, peak, denom = merged
        rows = out_block.shape[0]
        heads = peak.shape[0]
        return (out_block.reshape(rows, heads, -1) / denom.T[:, :, None]).reshape(rows, -1).astype(jnp.bfloat16)

    result = lax.map(one_block, jnp.arange(N_CTX, dtype=jnp.int32))
    return result.reshape(SEQ, -1)
```

```python
import jax
import jax.numpy as jnp
from jax import lax
from jax.experimental import pallas as pl
from jax.experimental.pallas import tpu as pltpu
from jax.sharding import PartitionSpec as P

HEAD_DIM = 128
KV_HEADS = 8
SHARE = 4
ROWS = 128
AXES = ("ctx", "head")
SCALE = HEAD_DIM**-0.5
LOG2E = 1.4426950408889634
HIDDEN = 1e30


def pairs_from(cycle, source):
    pairs = []
    for c in range(cycle):
        for h in range(2):
            origin = source(c, h)
            if origin is not None:
                pairs.append((origin[0] % cycle * 2 + origin[1], c * 2 + h))
    return pairs


def send(array, pairs):
    return lax.ppermute(array, AXES, pairs)


def attend(flags, q_ref, keys, values, out_ref):
    count = len(keys)
    ones = jnp.ones((ROWS * count, HEAD_DIM), jnp.bfloat16)
    row = lax.broadcasted_iota(jnp.int32, (SHARE * ROWS, ROWS), 0) % ROWS
    col = lax.broadcasted_iota(jnp.int32, (SHARE * ROWS, ROWS), 1)
    below = col <= row

    def group(g, carry):
        kv = pl.ds(pl.multiple_of(g * HEAD_DIM, HEAD_DIM), HEAD_DIM)
        q = jnp.concatenate(
            [
                q_ref[:, pl.ds(pl.multiple_of((g * SHARE + s) * HEAD_DIM, HEAD_DIM), HEAD_DIM)]
                for s in range(SHARE)
            ],
            axis=0,
        )
        scores = []
        top = None
        for j in range(count):
            part = lax.dot_general(
                q, keys[j][:, kv], (((1,), (1,)), ((), ())), preferred_element_type=jnp.float32
            )
            if j == 0:
                part = jnp.where(below, part, -HIDDEN)
                peak = jnp.max(part, axis=1, keepdims=True)
                top = peak
            else:
                peak = jnp.max(part, axis=1, keepdims=True)
                top = jnp.maximum(top, jnp.where(flags[j] > 0, peak, -HIDDEN))
            scores.append(part)
        weights = []
        for j in range(count):
            shift = top if j == 0 else jnp.where(flags[j] > 0, top, HIDDEN)
            weights.append(jnp.exp2((scores[j] - shift) * (SCALE * LOG2E)).astype(jnp.bfloat16))
        weights = jnp.concatenate(weights, axis=1)
        v = jnp.concatenate([values[j][:, kv] for j in range(count)], axis=0)
        both = jnp.dot(
            weights, jnp.concatenate([v, ones], axis=1), preferred_element_type=jnp.float32
        )
        mixed = (both[:, :HEAD_DIM] / both[:, HEAD_DIM:]).astype(jnp.bfloat16)
        for s in range(SHARE):
            out_ref[:, pl.ds(pl.multiple_of((g * SHARE + s) * HEAD_DIM, HEAD_DIM), HEAD_DIM)] = (
                mixed[s * ROWS : (s + 1) * ROWS]
            )
        return carry

    lax.fori_loop(0, KV_HEADS, group, 0)


def whole(flags_ref, q_ref, *refs):
    out_ref, k_pick, v_pick = refs[-3], refs[-2], refs[-1]
    tiles = refs[:-3]
    keys = [tiles[i] for i in range(6)]
    values = [tiles[10 + i] for i in range(6)]
    core = flags_ref[8]

    @pl.when(core == 0)
    def _():
        for n in range(2):
            k_pick[n] = tiles[6 + n][...]
            v_pick[n] = tiles[16 + n][...]

    @pl.when(core != 0)
    def _():
        for n in range(2):
            k_pick[n] = tiles[8 + n][...]
            v_pick[n] = tiles[18 + n][...]

    keys += [k_pick.at[0], k_pick.at[1]]
    values += [v_pick.at[0], v_pick.at[1]]
    flags = [flags_ref[j] for j in range(8)]
    attend(flags, q_ref, keys, values, out_ref)


def shards(queries, keys, values, block_place):
    cycle = lax.axis_size("ctx")
    routes = {
        "pair": pairs_from(cycle, lambda c, h: (c, 1 - h)),
        "next": pairs_from(cycle, lambda c, h: (c + 2, h)),
        "core": pairs_from(cycle, lambda c, h: (c ^ 1, h)),
        "down": pairs_from(cycle, lambda c, h: (c + 1, h) if c % 2 == 0 else None),
        "far": pairs_from(cycle, lambda c, h: (c + 1, h) if c % 2 == 1 else None),
        "cross": pairs_from(cycle, lambda c, h: (c + 1, 1 - h) if c % 2 == 1 else None),
    }

    def spread(a):
        b = send(a, routes["pair"])
        c = send(a, routes["next"])
        d = send(a, routes["down"])
        e = send(b, routes["down"])
        f = send(c, routes["core"])
        g = send(c, routes["pair"])
        far = send(c, routes["far"])
        cross = send(c, routes["cross"])
        j = send(g, routes["core"])
        return [a, b, c, f, g, j, d, e, far, cross]

    c = lax.axis_index("ctx")
    h = lax.axis_index("head")
    core = c % 2
    mate = c + 1 - 2 * core
    blocks = jnp.stack([c, c, c + 2, mate + 2, c + 2, mate + 2, c + 1 + 2 * core, c + 1 + 2 * core])
    halves = jnp.stack([h, 1 - h, h, h, 1 - h, 1 - h, h, 1 - h])
    place = block_place[(blocks % cycle) * 2 + halves]
    own = block_place[2 * c + h]
    flags = jnp.concatenate([(place < own).astype(jnp.int32), core[None].astype(jnp.int32)])
    vmem = pl.BlockSpec(memory_space=pltpu.VMEM)
    return pl.pallas_call(
        whole,
        out_shape=jax.ShapeDtypeStruct(queries.shape, queries.dtype),
        in_specs=[pl.BlockSpec(memory_space=pltpu.SMEM)] + [vmem] * 21,
        out_specs=vmem,
        scratch_shapes=[
            pltpu.VMEM((2, ROWS, KV_HEADS * HEAD_DIM), jnp.bfloat16),
            pltpu.VMEM((2, ROWS, KV_HEADS * HEAD_DIM), jnp.bfloat16),
        ],
        compiler_params=pltpu.CompilerParams(vmem_limit_bytes=40 * 1024 * 1024),
        cost_estimate=pl.CostEstimate(flops=2 * 10**9, bytes_accessed=6 * 2**20, transcendentals=2**22),
    )(flags, queries, *spread(keys), *spread(values))


def solution(mesh):
    spec = P(AXES, None)
    return jax.shard_map(
        shards, mesh=mesh, in_specs=(spec, spec, spec, P()), out_specs=spec, check_vma=False
    )
```

```python
import jax
import jax.numpy as jnp
from jax import lax
from jax.experimental import pallas as pl
from jax.experimental.pallas import tpu as pltpu
from jax.sharding import PartitionSpec as P

HEAD_DIM = 128
KV_HEADS = 8
SHARE = 4
ROWS = 128
AXES = ("ctx", "head")
SCALE2 = HEAD_DIM**-0.5 * 1.4426950408889634
HIDDEN = 1e30


def pairs_from(cycle, source):
    pairs = []
    for c in range(cycle):
        for h in range(2):
            origin = source(c, h)
            pairs.append((origin[0] % cycle * 2 + origin[1], c * 2 + h))
    return pairs


def send(array, pairs):
    return lax.ppermute(array, AXES, pairs)


def after(array, *others):
    return lax.optimization_barrier((array, *others))[0]


def lanes(index):
    return pl.ds(pl.multiple_of(index * HEAD_DIM, HEAD_DIM), HEAD_DIM)


def window(q, k, v, flags, own, top):
    parts = lax.dot_general(q, k, (((1,), (1,)), ((), ())), preferred_element_type=jnp.float32)
    parts = [parts[:, j * ROWS : (j + 1) * ROWS] for j in range(len(flags))]
    largest = None
    for j, part in enumerate(parts):
        if j == own:
            row = lax.broadcasted_iota(jnp.int32, part.shape, 0)
            col = lax.broadcasted_iota(jnp.int32, part.shape, 1)
            part = parts[j] = jnp.where(col <= row, part, -HIDDEN)
        else:
            part = part + jnp.where(flags[j], 0.0, -HIDDEN)
        largest = part if largest is None else jnp.maximum(largest, part)
    peak = jnp.broadcast_to(jnp.max(largest, axis=1, keepdims=True), (ROWS, HEAD_DIM))
    peak = peak if top is None else jnp.maximum(peak, top)
    weights = []
    for j, part in enumerate(parts):
        shift = peak if j == own else jnp.where(flags[j], peak, HIDDEN)
        weights.append(jnp.exp2((part - shift) * SCALE2).astype(jnp.bfloat16))
    both = jnp.dot(jnp.concatenate(weights, axis=1), v, preferred_element_type=jnp.float32)
    return both[:, :HEAD_DIM], both[:, HEAD_DIM:], peak


def with_ones(values):
    v = jnp.concatenate(values, axis=0)
    return jnp.concatenate([v, jnp.ones_like(v)], axis=1)


def merge(k_hbm, v_hbm, out_ref, sems):
    copies = [
        pltpu.make_async_copy(k_hbm, out_ref.at[:ROWS], sems.at[0]),
        pltpu.make_async_copy(v_hbm, out_ref.at[ROWS:], sems.at[1]),
    ]
    for copy in copies:
        copy.start()
    for copy in copies:
        copy.wait()


def visible(place_ref, slots):
    cycle = lax.axis_size("ctx")
    x = lax.axis_index("ctx")
    y = lax.axis_index("head")
    odd = x & 1
    closing = jnp.where((x & (cycle // 2 - 1)) >= cycle // 2 - 2, 1, 0)
    mine = y ^ (closing & odd)
    theirs = y ^ (closing & (1 - odd))
    mate = x + 1 - 2 * odd
    far = x + 1 + 2 * odd
    table = dict(
        a=(x, y), b=(x, 1 - y), c=(x + 2, mine), f=(mate + 2, theirs),
        g=(x + 2, 1 - mine), j=(mate + 2, 1 - theirs), d=(far, y), e=(far, 1 - y),
    )
    own = place_ref[2 * x + y]
    return [place_ref[2 * (table[s][0] & (cycle - 1)) + table[s][1]] < own for s in slots]


def early(place_ref, q_ref, a, b, c, f, out_ref, sum_ref, top_ref):
    tiles = [a, b, c, f]
    flags = visible(place_ref, 'abcf')

    def group(g, carry):
        k = jnp.concatenate([t[:ROWS, lanes(g)] for t in tiles], axis=0)
        v = with_ones([t[ROWS:, lanes(g)] for t in tiles])
        for s in range(SHARE):
            at = lanes(g * SHARE + s)
            out_ref[:, at], sum_ref[:, at], top_ref[:, at] = window(q_ref[:, at], k, v, flags, 0, None)
        return carry

    lax.fori_loop(0, KV_HEADS, group, 0, unroll=2)


def late(place_ref, q_ref, g_, j_, d, e, h, i, out1, sum1, top1, out_ref):
    flags = visible(place_ref, 'gjde')
    first = (lax.axis_index('ctx') & 1) == 0

    def group(g, carry):
        at = lanes(g)
        k = [g_[:ROWS, at], j_[:ROWS, at], jnp.where(first, d[:ROWS, at], h[:ROWS, at]), jnp.where(first, e[:ROWS, at], i[:ROWS, at])]
        v = [g_[ROWS:, at], j_[ROWS:, at], jnp.where(first, d[ROWS:, at], h[ROWS:, at]), jnp.where(first, e[ROWS:, at], i[ROWS:, at])]
        k = jnp.concatenate(k, axis=0)
        v = with_ones(v)
        for s in range(SHARE):
            at = lanes(g * SHARE + s)
            out, total, peak = window(q_ref[:, at], k, v, flags, None, top1[:, at])
            keep = jnp.exp2((top1[:, at] - peak) * SCALE2)
            out = out1[:, at] * keep + out
            total = sum1[:, at] * keep + total
            out_ref[:, at] = (out / total).astype(jnp.bfloat16)
        return carry

    lax.fori_loop(0, KV_HEADS, group, 0, unroll=2)


SMEM = pl.BlockSpec(memory_space=pltpu.SMEM)
VMEM = pl.BlockSpec(memory_space=pltpu.VMEM)
PARAMS = pltpu.CompilerParams(vmem_limit_bytes=40 * 2**20)
COST = pl.CostEstimate(flops=2**30, bytes_accessed=3 * 2**20, transcendentals=2**21)


def shards(queries, keys, values, block_place):
    cycle = lax.axis_size("ctx")

    def closing(c):
        return c % (cycle // 2) >= cycle // 2 - 2

    def next_half(c, h):
        return 1 - h if closing(c) and c % 2 == 1 else h

    pair = pairs_from(cycle, lambda c, h: (c, 1 - h))
    ahead = pairs_from(cycle, lambda c, h: (c + 2, next_half(c, h)))
    core = pairs_from(cycle, lambda c, h: (c ^ 1, h))
    one = pairs_from(cycle, lambda c, h: (c + 1, h))
    cross = pairs_from(cycle, lambda c, h: (c + 1, 1 - h) if c % 2 == 1 else (c + 1, h))

    a = pl.pallas_call(
        merge,
        out_shape=pltpu.VMEM((2 * ROWS, keys.shape[1]), keys.dtype),
        in_specs=[pl.BlockSpec(memory_space=pl.ANY)] * 2,
        out_specs=VMEM,
        scratch_shapes=[pltpu.SemaphoreType.DMA((2,))],
    )(keys, values)
    b = send(a, pair)
    c = send(a, ahead)
    f = send(c, core)
    g = send(c, pair)
    h = send(c, one)
    i = send(c, cross)
    d = send(after(a, c), core)
    e = send(after(b, c), core)

    full = pltpu.VMEM(queries.shape, jnp.float32)
    state = pl.pallas_call(
        early,
        out_shape=[full] * 3,
        in_specs=[SMEM] + [VMEM] * 5,
        out_specs=[VMEM] * 3,
        compiler_params=PARAMS,
        cost_estimate=COST,
    )(block_place, queries, a, b, c, f)
    j = send(after(g, *state), core)
    return pl.pallas_call(
        late,
        out_shape=jax.ShapeDtypeStruct(queries.shape, queries.dtype),
        in_specs=[SMEM] + [VMEM] * 10,
        out_specs=VMEM,
        compiler_params=PARAMS,
        cost_estimate=COST,
    )(block_place, queries, g, j, d, e, h, i, *state)


def solution(mesh):
    spec = P(AXES, None)
    return jax.shard_map(
        shards, mesh=mesh, in_specs=(spec, spec, spec, P()), out_specs=spec, check_vma=False
    )
```

```python
import jax
import jax.numpy as jnp
from jax import lax
from jax.experimental import pallas as pl
from jax.experimental.pallas import tpu as pltpu
from jax.sharding import PartitionSpec as P

HEAD_DIM = 128
KV_HEADS = 8
SHARE = 4
ROWS = 128
AXES = ("ctx", "head")
SCALE2 = HEAD_DIM**-0.5 * 1.4426950408889634
HIDDEN = 1e30


def pairs_from(cycle, source):
    pairs = []
    for c in range(cycle):
        for h in range(2):
            origin = source(c, h)
            pairs.append((origin[0] % cycle * 2 + origin[1], c * 2 + h))
    return pairs


def send(array, pairs):
    return lax.ppermute(array, AXES, pairs)


def after(array, *others):
    return lax.optimization_barrier((array, *others))[0]


def lanes(first, count=1):
    return slice(first * HEAD_DIM, (first + count) * HEAD_DIM)


def with_ones(values):
    v = jnp.concatenate(values, axis=0)
    return jnp.concatenate([v, jnp.ones_like(v)], axis=1)


def products(g, q_ref, keys, scores):
    q = jnp.concatenate([q_ref[:, lanes(g * SHARE + s)] for s in range(SHARE)], axis=0)
    k = jnp.concatenate(keys, axis=0)
    scores[g % 2] = lax.dot_general(q, k, (((1,), (1,)), ((), ())), preferred_element_type=jnp.float32)


def soften(g, s, scores, weights, flags, own, top):
    rows = slice(s * ROWS, (s + 1) * ROWS)
    parts = [scores[g % 2, rows, lanes(j)] for j in range(len(flags))]
    largest = None
    for j, part in enumerate(parts):
        if j == own:
            row = lax.broadcasted_iota(jnp.int32, part.shape, 0)
            col = lax.broadcasted_iota(jnp.int32, part.shape, 1)
            part = parts[j] = jnp.where(col <= row, part, -HIDDEN)
        else:
            part = part + jnp.where(flags[j], 0.0, -HIDDEN)
        largest = part if largest is None else jnp.maximum(largest, part)
    peak = jnp.broadcast_to(jnp.max(largest, axis=1, keepdims=True), (ROWS, HEAD_DIM))
    peak = peak if top is None else jnp.maximum(peak, top)
    for j, part in enumerate(parts):
        shift = peak if j == own else jnp.where(flags[j], peak, HIDDEN)
        weights[g % 2, rows, lanes(j)] = jnp.exp2((part - shift) * SCALE2).astype(jnp.bfloat16)
    return peak


def staged(first, second, third):
    for step in range(KV_HEADS + 2):
        if step >= 2:
            third(step - 2)
        if 1 <= step <= KV_HEADS:
            second(step - 1)
        if step < KV_HEADS:
            first(step)


def merge(k_hbm, v_hbm, out_ref, sems):
    copies = [
        pltpu.make_async_copy(k_hbm, out_ref.at[:ROWS], sems.at[0]),
        pltpu.make_async_copy(v_hbm, out_ref.at[ROWS:], sems.at[1]),
    ]
    for copy in copies:
        copy.start()
    for copy in copies:
        copy.wait()


def visible(place_ref, slots):
    cycle = lax.axis_size("ctx")
    x = lax.axis_index("ctx")
    y = lax.axis_index("head")
    odd = x & 1
    closing = jnp.where((x & (cycle // 2 - 1)) >= cycle // 2 - 2, 1, 0)
    mine = y ^ (closing & odd)
    theirs = y ^ (closing & (1 - odd))
    mate = x + 1 - 2 * odd
    far = x + 1 + 2 * odd
    table = dict(
        a=(x, y), b=(x, 1 - y), c=(x + 2, mine), f=(mate + 2, theirs),
        g=(x + 2, 1 - mine), j=(mate + 2, 1 - theirs), d=(far, y), e=(far, 1 - y),
    )
    own = place_ref[2 * x + y]
    return [place_ref[2 * (table[s][0] & (cycle - 1)) + table[s][1]] < own for s in slots]


def early(place_ref, q_ref, a, b, out_ref, sum_ref, top_ref, scores, weights):
    tiles = [a, b]
    flags = visible(place_ref, "ab")

    def first(g):
        products(g, q_ref, [t[:ROWS, lanes(g)] for t in tiles], scores)

    def second(g):
        for s in range(SHARE):
            top_ref[:, lanes(g * SHARE + s)] = soften(g, s, scores, weights, flags, 0, None)

    def third(g):
        v = with_ones([t[ROWS:, lanes(g)] for t in tiles])
        both = jnp.dot(weights[g % 2], v, preferred_element_type=jnp.float32)
        for s in range(SHARE):
            rows = slice(s * ROWS, (s + 1) * ROWS)
            out_ref[:, lanes(g * SHARE + s)] = both[rows, :HEAD_DIM]
            sum_ref[:, lanes(g * SHARE + s)] = both[rows, HEAD_DIM:]

    staged(first, second, third)


def middle(place_ref, q_ref, c, f, out1, sum1, top1, out_ref, sum_ref, top_ref, scores, weights, keep):
    tiles = [c, f]
    flags = visible(place_ref, "cf")

    def first(g):
        products(g, q_ref, [t[:ROWS, lanes(g)] for t in tiles], scores)

    def second(g):
        for s in range(SHARE):
            at = lanes(g * SHARE + s)
            peak = soften(g, s, scores, weights, flags, None, top1[:, at])
            keep[g % 2, s * ROWS : (s + 1) * ROWS] = jnp.exp2((top1[:, at] - peak) * SCALE2)
            top_ref[:, at] = peak

    def third(g):
        v = with_ones([t[ROWS:, lanes(g)] for t in tiles])
        both = jnp.dot(weights[g % 2], v, preferred_element_type=jnp.float32)
        for s in range(SHARE):
            at = lanes(g * SHARE + s)
            rows = slice(s * ROWS, (s + 1) * ROWS)
            factor = keep[g % 2, rows]
            out_ref[:, at] = out1[:, at] * factor + both[rows, :HEAD_DIM]
            sum_ref[:, at] = sum1[:, at] * factor + both[rows, HEAD_DIM:]

    staged(first, second, third)


def late(place_ref, q_ref, g_, j_, d, e, h, i, out1, sum1, top1, out_hbm, scores, weights, keep, out_ref, sems):
    flags = visible(place_ref, "gjde")
    even = (lax.axis_index("ctx") & 1) == 0

    def tiles(rows, at):
        return [g_[rows, at], j_[rows, at], jnp.where(even, d[rows, at], h[rows, at]), jnp.where(even, e[rows, at], i[rows, at])]

    def leave(g):
        at = lanes(g * SHARE, SHARE)
        return pltpu.make_async_copy(out_ref.at[:, at], out_hbm.at[:, at], sems.at[g])

    def first(g):
        products(g, q_ref, tiles(slice(0, ROWS), lanes(g)), scores)

    def second(g):
        for s in range(SHARE):
            top = top1[:, lanes(g * SHARE + s)]
            peak = soften(g, s, scores, weights, flags, None, top)
            keep[g % 2, s * ROWS : (s + 1) * ROWS] = jnp.exp2((top - peak) * SCALE2)

    def third(g):
        v = with_ones(tiles(slice(ROWS, 2 * ROWS), lanes(g)))
        both = jnp.dot(weights[g % 2], v, preferred_element_type=jnp.float32)
        for s in range(SHARE):
            at = lanes(g * SHARE + s)
            rows = slice(s * ROWS, (s + 1) * ROWS)
            factor = keep[g % 2, rows]
            out = out1[:, at] * factor + both[rows, :HEAD_DIM]
            total = sum1[:, at] * factor + both[rows, HEAD_DIM:]
            out_ref[:, at] = (out / total).astype(jnp.bfloat16)
        leave(g).start()

    staged(first, second, third)
    for g in range(KV_HEADS):
        leave(g).wait()


SMEM = pl.BlockSpec(memory_space=pltpu.SMEM)
VMEM = pl.BlockSpec(memory_space=pltpu.VMEM)
def work(tiles):
    return [
        pltpu.VMEM((2, SHARE * ROWS, tiles * ROWS), jnp.float32),
        pltpu.VMEM((2, SHARE * ROWS, tiles * ROWS), jnp.bfloat16),
    ]


KEEP = pltpu.VMEM((2, SHARE * ROWS, HEAD_DIM), jnp.float32)
PARAMS = pltpu.CompilerParams(vmem_limit_bytes=16 * 2**20)
COST = pl.CostEstimate(flops=2**30, bytes_accessed=3 * 2**20, transcendentals=2**21)


def shards(queries, keys, values, block_place):
    cycle = lax.axis_size("ctx")

    def closing(c):
        return c % (cycle // 2) >= cycle // 2 - 2

    def next_half(c, h):
        return 1 - h if closing(c) and c % 2 == 1 else h

    pair = pairs_from(cycle, lambda c, h: (c, 1 - h))
    ahead = pairs_from(cycle, lambda c, h: (c + 2, next_half(c, h)))
    core = pairs_from(cycle, lambda c, h: (c ^ 1, h))
    one = pairs_from(cycle, lambda c, h: (c + 1, h))
    cross = pairs_from(cycle, lambda c, h: (c + 1, 1 - h) if c % 2 == 1 else (c + 1, h))

    a = pl.pallas_call(
        merge,
        out_shape=pltpu.VMEM((2 * ROWS, keys.shape[1]), keys.dtype),
        in_specs=[pl.BlockSpec(memory_space=pl.ANY)] * 2,
        out_specs=VMEM,
        scratch_shapes=[pltpu.SemaphoreType.DMA((2,))],
    )(keys, values)
    b = send(a, pair)
    c = send(a, ahead)
    f = send(c, core)
    g = send(c, pair)

    full = pltpu.VMEM(queries.shape, jnp.float32)
    state = pl.pallas_call(
        early,
        out_shape=[full] * 3,
        in_specs=[SMEM] + [VMEM] * 3,
        out_specs=[VMEM] * 3,
        scratch_shapes=work(2),
        compiler_params=PARAMS,
        cost_estimate=COST,
    )(block_place, queries, a, b)
    c2 = after(c, *state)
    h = send(c2, one)
    i = send(c2, cross)
    state = pl.pallas_call(
        middle,
        out_shape=[full] * 3,
        in_specs=[SMEM] + [VMEM] * 6,
        out_specs=[VMEM] * 3,
        scratch_shapes=work(2) + [KEEP],
        compiler_params=PARAMS,
        cost_estimate=COST,
    )(block_place, queries, c, f, *state)
    d = send(after(a, *state), core)
    e = send(after(b, *state), core)
    j = send(after(g, *state), core)
    return pl.pallas_call(
        late,
        out_shape=jax.ShapeDtypeStruct(queries.shape, queries.dtype),
        in_specs=[SMEM] + [VMEM] * 10,
        out_specs=pl.BlockSpec(memory_space=pl.ANY),
        scratch_shapes=work(4)
        + [
            pltpu.VMEM((2, SHARE * ROWS, HEAD_DIM), jnp.float32),
            pltpu.VMEM(queries.shape, queries.dtype),
            pltpu.SemaphoreType.DMA((KV_HEADS,)),
        ],
        compiler_params=PARAMS,
        cost_estimate=COST,
    )(block_place, queries, g, j, d, e, h, i, *state)


def solution(mesh):
    spec = P(AXES, None)
    return jax.shard_map(
        shards, mesh=mesh, in_specs=(spec, spec, spec, P()), out_specs=spec, check_vma=False
    )
```

```python
import jax
import jax.numpy as jnp
from jax import lax
from jax.experimental import pallas as pl
from jax.experimental.pallas import tpu as pltpu
from jax.sharding import PartitionSpec as P

HEAD_DIM = 128
KV_HEADS = 8
SHARE = 4
ROWS = 128
AXES = ("ctx", "head")
SCALE2 = HEAD_DIM**-0.5 * 1.4426950408889634
HIDDEN = 1e30


def pairs_from(cycle, source):
    pairs = []
    for c in range(cycle):
        for h in range(2):
            origin = source(c, h)
            pairs.append((origin[0] % cycle * 2 + origin[1], c * 2 + h))
    return pairs


def send(array, pairs):
    return lax.ppermute(array, AXES, pairs)


def after(array, *others):
    return lax.optimization_barrier((array, *others))[0]


def lanes(first, count=1):
    return slice(first * HEAD_DIM, (first + count) * HEAD_DIM)


def with_ones(values):
    v = jnp.concatenate(values, axis=0)
    return jnp.concatenate([v, jnp.ones_like(v)], axis=1)


def products(g, q_ref, keys, scores):
    q = jnp.concatenate([q_ref[:, lanes(g * SHARE + s)] for s in range(SHARE)], axis=0)
    k = jnp.concatenate(keys, axis=0)
    scores[g % 2] = lax.dot_general(q, k, (((1,), (1,)), ((), ())), preferred_element_type=jnp.float32)


def soften(g, s, scores, weights, flags, own, top):
    rows = slice(s * ROWS, (s + 1) * ROWS)
    parts = [scores[g % 2, rows, lanes(j)] for j in range(len(flags))]
    largest = None
    for j, part in enumerate(parts):
        if j == own:
            row = lax.broadcasted_iota(jnp.int32, part.shape, 0)
            col = lax.broadcasted_iota(jnp.int32, part.shape, 1)
            part = parts[j] = jnp.where(col <= row, part, -HIDDEN)
        else:
            part = part + jnp.where(flags[j], 0.0, -HIDDEN)
        largest = part if largest is None else jnp.maximum(largest, part)
    peak = jnp.broadcast_to(jnp.max(largest, axis=1, keepdims=True), (ROWS, HEAD_DIM))
    peak = peak if top is None else jnp.maximum(peak, top)
    for j, part in enumerate(parts):
        shift = peak if j == own else jnp.where(flags[j], peak, HIDDEN)
        weights[g % 2, rows, lanes(j)] = jnp.exp2((part - shift) * SCALE2).astype(jnp.bfloat16)
    return peak


def staged(first, second, third):
    for step in range(KV_HEADS + 2):
        if step >= 2:
            third(step - 2)
        if 1 <= step <= KV_HEADS:
            second(step - 1)
        if step < KV_HEADS:
            first(step)


def merge(k_hbm, v_hbm, out_ref, sems):
    part = ROWS // 4
    copies = [
        pltpu.make_async_copy(
            ref.at[pl.ds(n * part, part)], out_ref.at[pl.ds(base + n * part, part)], sems.at[base // part + n]
        )
        for ref, base in ((k_hbm, 0), (v_hbm, ROWS))
        for n in range(4)
    ]
    for copy in copies:
        copy.start()
    for copy in copies:
        copy.wait()


def visible(place_ref, slots):
    cycle = lax.axis_size("ctx")
    x = lax.axis_index("ctx")
    y = lax.axis_index("head")
    odd = x & 1
    closing = jnp.where((x & (cycle // 2 - 1)) >= cycle // 2 - 2, 1, 0)
    mine = y ^ (closing & odd)
    theirs = y ^ (closing & (1 - odd))
    mate = x + 1 - 2 * odd
    far = x + 1 + 2 * odd
    table = dict(
        a=(x, y), b=(x, 1 - y), c=(x + 2, mine), f=(mate + 2, theirs),
        g=(x + 2, 1 - mine), j=(mate + 2, 1 - theirs), d=(far, y), e=(far, 1 - y),
    )
    own = place_ref[2 * x + y]
    return [place_ref[2 * (table[s][0] & (cycle - 1)) + table[s][1]] < own for s in slots]


def early(place_ref, q_ref, a, c, out_ref, sum_ref, top_ref, scores, weights):
    tiles = [a, c]
    flags = visible(place_ref, "ac")

    def first(g):
        products(g, q_ref, [t[:ROWS, lanes(g)] for t in tiles], scores)

    def second(g):
        for s in range(SHARE):
            top_ref[:, lanes(g * SHARE + s)] = soften(g, s, scores, weights, flags, 0, None)

    def third(g):
        v = with_ones([t[ROWS:, lanes(g)] for t in tiles])
        both = jnp.dot(weights[g % 2], v, preferred_element_type=jnp.float32)
        for s in range(SHARE):
            rows = slice(s * ROWS, (s + 1) * ROWS)
            out_ref[:, lanes(g * SHARE + s)] = both[rows, :HEAD_DIM]
            sum_ref[:, lanes(g * SHARE + s)] = both[rows, HEAD_DIM:]

    staged(first, second, third)


def middle(place_ref, q_ref, b, f, out1, sum1, top1, out_ref, sum_ref, top_ref, scores, weights, keep):
    tiles = [b, f]
    flags = visible(place_ref, "bf")

    def first(g):
        products(g, q_ref, [t[:ROWS, lanes(g)] for t in tiles], scores)

    def second(g):
        for s in range(SHARE):
            at = lanes(g * SHARE + s)
            peak = soften(g, s, scores, weights, flags, None, top1[:, at])
            keep[g % 2, s * ROWS : (s + 1) * ROWS] = jnp.exp2((top1[:, at] - peak) * SCALE2)
            top_ref[:, at] = peak

    def third(g):
        v = with_ones([t[ROWS:, lanes(g)] for t in tiles])
        both = jnp.dot(weights[g % 2], v, preferred_element_type=jnp.float32)
        for s in range(SHARE):
            at = lanes(g * SHARE + s)
            rows = slice(s * ROWS, (s + 1) * ROWS)
            factor = keep[g % 2, rows]
            out_ref[:, at] = out1[:, at] * factor + both[rows, :HEAD_DIM]
            sum_ref[:, at] = sum1[:, at] * factor + both[rows, HEAD_DIM:]

    staged(first, second, third)


def finish(place_ref, q_ref, g_, j_, near, far, out1, sum1, top1, out_hbm, scores, weights, keep, out_ref, sems):
    flags = visible(place_ref, "gjde")

    def tiles(rows, at):
        return [t[rows, at] for t in (g_, j_, near, far)]

    def leave(g):
        at = lanes(g * SHARE, SHARE)
        return pltpu.make_async_copy(out_ref.at[:, at], out_hbm.at[:, at], sems.at[g])

    def first(g):
        products(g, q_ref, tiles(slice(0, ROWS), lanes(g)), scores)

    def second(g):
        for s in range(SHARE):
            top = top1[:, lanes(g * SHARE + s)]
            peak = soften(g, s, scores, weights, flags, None, top)
            keep[g % 2, s * ROWS : (s + 1) * ROWS] = jnp.exp2((top - peak) * SCALE2)

    def third(g):
        v = with_ones(tiles(slice(ROWS, 2 * ROWS), lanes(g)))
        both = jnp.dot(weights[g % 2], v, preferred_element_type=jnp.float32)
        for s in range(SHARE):
            at = lanes(g * SHARE + s)
            rows = slice(s * ROWS, (s + 1) * ROWS)
            factor = keep[g % 2, rows]
            out = out1[:, at] * factor + both[rows, :HEAD_DIM]
            total = sum1[:, at] * factor + both[rows, HEAD_DIM:]
            out_ref[:, at] = (out / total).astype(jnp.bfloat16)
        leave(g).start()

    staged(first, second, third)
    for g in range(KV_HEADS):
        leave(g).wait()


def late(place_ref, q_ref, g_, j_, d, e, h, i, *rest):
    even = (lax.axis_index("ctx") & 1) == 0

    @pl.when(even)
    def _():
        finish(place_ref, q_ref, g_, j_, d, e, *rest)

    @pl.when(jnp.logical_not(even))
    def _():
        finish(place_ref, q_ref, g_, j_, h, i, *rest)


SMEM = pl.BlockSpec(memory_space=pltpu.SMEM)
VMEM = pl.BlockSpec(memory_space=pltpu.VMEM)
def work(tiles):
    return [
        pltpu.VMEM((2, SHARE * ROWS, tiles * ROWS), jnp.float32),
        pltpu.VMEM((2, SHARE * ROWS, tiles * ROWS), jnp.bfloat16),
    ]


KEEP = pltpu.VMEM((2, SHARE * ROWS, HEAD_DIM), jnp.float32)
PARAMS = pltpu.CompilerParams(vmem_limit_bytes=16 * 2**20)
COST = pl.CostEstimate(flops=2**30, bytes_accessed=3 * 2**20, transcendentals=2**21)


def shards(queries, keys, values, block_place):
    cycle = lax.axis_size("ctx")

    def closing(c):
        return c % (cycle // 2) >= cycle // 2 - 2

    def next_half(c, h):
        return 1 - h if closing(c) and c % 2 == 1 else h

    pair = pairs_from(cycle, lambda c, h: (c, 1 - h))
    ahead = pairs_from(cycle, lambda c, h: (c + 2, next_half(c, h)))
    core = pairs_from(cycle, lambda c, h: (c ^ 1, h))
    one = pairs_from(cycle, lambda c, h: (c + 1, h))
    cross = pairs_from(cycle, lambda c, h: (c + 1, 1 - h) if c % 2 == 1 else (c + 1, h))

    a = pl.pallas_call(
        merge,
        out_shape=pltpu.VMEM((2 * ROWS, keys.shape[1]), keys.dtype),
        in_specs=[pl.BlockSpec(memory_space=pl.ANY)] * 2,
        out_specs=VMEM,
        scratch_shapes=[pltpu.SemaphoreType.DMA((8,))],
    )(keys, values)
    b = send(a, pair)
    c = send(a, ahead)
    f = send(c, core)
    g = send(c, pair)

    full = pltpu.VMEM(queries.shape, jnp.float32)
    state = pl.pallas_call(
        early,
        out_shape=[full] * 3,
        in_specs=[SMEM] + [VMEM] * 3,
        out_specs=[VMEM] * 3,
        scratch_shapes=work(2),
        compiler_params=PARAMS,
        cost_estimate=COST,
    )(block_place, queries, a, c)
    d = send(after(a, *state), core)
    e = send(after(b, *state), core)
    c2 = after(c, *state)
    h = send(c2, one)
    i = send(c2, cross)
    state = pl.pallas_call(
        middle,
        out_shape=[full] * 3,
        in_specs=[SMEM] + [VMEM] * 6,
        out_specs=[VMEM] * 3,
        scratch_shapes=work(2) + [KEEP],
        compiler_params=PARAMS,
        cost_estimate=COST,
    )(block_place, queries, b, f, *state)
    j = send(after(g, *state), core)
    return pl.pallas_call(
        late,
        out_shape=jax.ShapeDtypeStruct(queries.shape, queries.dtype),
        in_specs=[SMEM] + [VMEM] * 10,
        out_specs=pl.BlockSpec(memory_space=pl.ANY),
        scratch_shapes=work(4)
        + [
            pltpu.VMEM((2, SHARE * ROWS, HEAD_DIM), jnp.float32),
            pltpu.VMEM(queries.shape, queries.dtype),
            pltpu.SemaphoreType.DMA((KV_HEADS,)),
        ],
        compiler_params=PARAMS,
        cost_estimate=COST,
    )(block_place, queries, g, j, d, e, h, i, *state)


def solution(mesh):
    spec = P(AXES, None)
    return jax.shard_map(
        shards, mesh=mesh, in_specs=(spec, spec, spec, P()), out_specs=spec, check_vma=False
    )
```
